32 devices in a mesh: dp: 4 (over y, x), expert: 8 (over z, core).
Axes of the slice: x: 2, y: 2, z: 4, core: 2. Of those that a mesh axis runs over, the one named last changes fastest.
Arguments:
- slot_grads: bfloat16 [4, 8, 384, 2048], P('dp', 'expert'), may hold values from -0.23925781 to 0.23925781
- momentum: float32 [384, 4, 2048], P('expert', None, 'dp'), may hold values from -0.16 to 0.16
- master_weights: float32 [384, 4, 2048], P('expert', None, 'dp'), may hold values from -0.3125 to 0.3125
- current_slots: int32 [8, 1], replicated, may hold values from 0 to 3
- next_slots: int32 [8, 1], replicated, may hold values from 0 to 3
- live_counts: int32 [4, 8], P('dp', 'expert'), may hold values from 1 to 512
- route_index: int32 [4, 8, 4, 128], P('dp', 'expert'), may hold values from 0 to 127, each once within a row
- activations: bfloat16 [4, 8, 512, 384], P('dp', 'expert'), may hold values from -6 to 6
Outputs:
- new_momentum: float32 [384, 4, 2048], P('expert', None, 'dp')
- expert_out: bfloat16 [4, 8, 512, 2048], P('dp', 'expert')
The draws below stay inside these ranges and needn't reach their ends.
Inputs may be any that keep to these rules, and one draw needn't show every extreme that they name: `current_slots`: every expert is held by at least one slot. `next_slots`: every expert is held by at least one slot. `route_index`: each block of 128 indices names every row of its block once.
All inputs are finite; a program needn't handle non-finite values.
Results may differ from the reference program's by a relative error of at most 0.015.
Values may be sent and summed in bfloat16 or wider, within the bound.
No kernel may reach another device: no remote copies, remote signals or barrier semaphores. Data moves between devices by JAX's collectives and lax.ppermute only.
A program may use at most 64 MiB of HBM per device.

```python
import jax
import jax.numpy as jnp
from jax import lax

D = 2048
FF_W = 384
QBLOCK = 128
RBLOCK = 128
ROWS = 512
EXPERTS = 4
SLOTS = 8
N_DP = 4


def set_ends(result, own_key, smallest, largest):
    extent = result.shape
    index_at = [jax.random.randint(jax.random.fold_in(own_key, axis), (), 0, extent[axis]) for axis in range(len(extent))]
    result = result.at[tuple(index_at)].set(smallest)
    longest = extent.index(max(extent))
    index_at[longest] = (index_at[longest] + 1) % extent[longest]
    return result.at[tuple(index_at)].set(largest)


def level_of(key, shape, shards, smallest, top_value):
    factor_of, own = 1.0, jax.random.fold_in(key, 6)
    for position, shards_of in shards:
        draws = jnp.exp(jax.random.uniform(jax.random.fold_in(own, position), (shards_of,), jnp.float32, smallest / len(shards), top_value / len(shards)))
        factor_of = factor_of * jnp.repeat(draws, shape[position] // shards_of).reshape([-1 if axis == position else 1 for axis in range(len(shape))])
    return factor_of


def distinct(key, rows, amount, top, lift):
    sequence = jax.random.permutation(jax.random.fold_in(key, 1), amount)
    boost = sequence
    for power in range(3):
        boost = boost * boost // amount
    boost = boost * lift // amount
    chance = jax.random.randint(jax.random.fold_in(key, 2), (rows, amount), 0, 4096) + boost
    fixed_rows = jax.random.permutation(jax.random.fold_in(key, 3), rows)[jnp.arange(amount) % rows]
    chance = jnp.where(jnp.arange(rows)[:, None] == fixed_rows[None, :], 1 << 14, chance)
    priority = chance * amount + jnp.arange(amount)
    return lax.top_k(priority.astype(jnp.int32), top)[1].astype(jnp.int32)


def gaussian(own_key, extent, width, limit, shards=(), kind=jnp.bfloat16):
    array = width * jax.random.normal(own_key, extent, jnp.float32)
    if shards:
        array = array * level_of(own_key, extent, shards, -0.22, 0.18)
    return jnp.clip(array, -limit, limit).astype(kind)


def setup_inputs(seed: int = 0) -> dict:
    splits = jax.random.split(jax.random.key(seed), 9)
    slot_grads = gaussian(splits[0], (N_DP, SLOTS, FF_W, D), 0.03, 0.23925781, ((0, 4), (1, 8)))
    momentum = gaussian(splits[1], (FF_W, EXPERTS, D), 0.02, 0.16, ((0, 8), (2, 4)), jnp.float32)
    master_weights = gaussian(splits[2], (FF_W, EXPERTS, D), FF_W ** -0.5, 0.3125, ((0, 8), (2, 4)), jnp.float32)
    current_slots = distinct(splits[3], SLOTS, EXPERTS, 1, 4096)
    next_slots = distinct(splits[4], SLOTS, EXPERTS, 1, 4096)
    live_counts = set_ends(jax.random.randint(splits[5], (N_DP, SLOTS), 1, ROWS + 1), jax.random.fold_in(splits[5], 1), 1, ROWS).astype(jnp.int32)
    route_index = jax.vmap(lambda own: jax.random.permutation(own, RBLOCK))(jax.random.split(splits[6], N_DP * SLOTS * (ROWS // RBLOCK))).reshape((N_DP, SLOTS, ROWS // RBLOCK, RBLOCK)).astype(jnp.int32)
    activations = gaussian(splits[7], (N_DP, SLOTS, ROWS, FF_W), 1.0, 6.0, ((0, 4), (1, 8)))
    return dict(slot_grads=slot_grads, momentum=momentum, master_weights=master_weights, current_slots=current_slots, next_slots=next_slots, live_counts=live_counts, route_index=route_index, activations=activations)


momentum_decay = 0.9
step_rate = 0.5
epsilon = 1e-6
range_limit = 448.0


def reference(slot_grads, momentum, master_weights, current_slots, next_slots, live_counts, route_index, activations):
    owners = current_slots[:, 0].astype(jnp.int32)

    def accumulate(slot_index, totals):
        slot_index = jnp.asarray(slot_index).astype(jnp.int32)
        taken = lax.dynamic_index_in_dim(slot_grads, slot_index, 1, keepdims=False)
        summed = jnp.sum(taken.astype(jnp.float32), axis=0)
        return totals.at[:, owners[slot_index], :].add(summed)

    totals = lax.fori_loop(0, SLOTS, accumulate, jnp.zeros((FF_W, EXPERTS, D), jnp.float32))
    new_momentum = momentum_decay * momentum + totals
    weights = master_weights - step_rate * new_momentum
    blocks = weights.reshape(FF_W, EXPERTS, D // QBLOCK, QBLOCK)
    previous = master_weights.reshape(FF_W, EXPERTS, D // QBLOCK, QBLOCK)
    scales = (jnp.max(jnp.abs(previous), axis=3) / range_limit + epsilon).astype(jnp.bfloat16)
    scaled = blocks / scales.astype(jnp.float32)[:, :, :, None]
    quantized = jnp.clip(scaled, -range_limit, range_limit).astype(jnp.bfloat16)
    restored = (quantized.astype(jnp.float32) * scales.astype(jnp.float32)[:, :, :, None]).astype(jnp.bfloat16)
    restored = restored.reshape(FF_W, EXPERTS, D)
    chosen = next_slots[:, 0].astype(jnp.int32)
    row_numbers = jnp.arange(ROWS, dtype=jnp.int32)

    def per_slot(slot_index):
        weight = lax.dynamic_index_in_dim(restored, chosen[slot_index], 1, keepdims=False)
        inputs = lax.dynamic_index_in_dim(activations, slot_index, 1, keepdims=False)
        indices = lax.dynamic_index_in_dim(route_index, slot_index, 1, keepdims=False)
        counts = lax.dynamic_index_in_dim(live_counts, slot_index, 1, keepdims=False)
        blocked = inputs.reshape(N_DP, ROWS // RBLOCK, RBLOCK, FF_W)
        selected = jnp.take_along_axis(blocked, indices[:, :, :, None], axis=2).reshape(N_DP * ROWS, FF_W)
        product = jnp.dot(selected, weight, preferred_element_type=jnp.float32).reshape(N_DP, ROWS, D)
        live = row_numbers[None, :] < counts[:, None]
        return jnp.where(live[:, :, None], product, 0.0).astype(jnp.bfloat16)

    outputs = lax.map(per_slot, jnp.arange(SLOTS, dtype=jnp.int32))
    expert_out = jnp.transpose(outputs, (1, 0, 2, 3))
    return new_momentum, expert_out
```

```python
import functools

import jax
import jax.numpy as jnp
from jax import lax
from jax.experimental import pallas as pl
from jax.experimental.pallas import tpu as pltpu
from jax.sharding import PartitionSpec as P

QBLOCK = 128
momentum_decay = 0.9
step_rate = 0.5
epsilon = 1e-06
range_limit = 448.0
f32, bf16 = jnp.float32, jnp.bfloat16


def select_kernel(live_ref, index_ref, act_ref, out_ref):
    blocks, size = index_ref.shape
    for q in range(blocks):
        rows = lax.broadcasted_iota(jnp.int32, (size, size), 0)
        hot = (rows == index_ref[q : q + 1, :]).astype(f32).astype(bf16)
        picked = lax.dot_general(
            hot, act_ref[q * size : (q + 1) * size, :], (((0,), (0,)), ((), ())), preferred_element_type=f32
        )
        at = lax.broadcasted_iota(jnp.int32, picked.shape, 0) + q * size
        out_ref[q * size : (q + 1) * size, :] = jnp.where(at < live_ref[0, 0], picked, 0.0).astype(bf16)


def select_rows(activations, route_index, live_counts):
    rows, hidden = activations.shape
    return pl.pallas_call(
        select_kernel,
        out_shape=jax.ShapeDtypeStruct((rows, hidden), bf16),
        in_specs=[
            pl.BlockSpec(memory_space=pltpu.SMEM),
            pl.BlockSpec(memory_space=pltpu.VMEM),
            pl.BlockSpec(memory_space=pltpu.VMEM),
        ],
        out_specs=pl.BlockSpec(memory_space=pltpu.VMEM),
    )(live_counts, route_index, activations)


def product_kernel(count_j, count_k, place_ref, sel_ref, *refs):
    pieces = refs[: count_j * count_k]
    out_ref, weight, result, sems = refs[count_j * count_k :]
    e, d = place_ref[0], place_ref[1]
    half = pieces[0].shape[0] // 2
    columns = pieces[0].shape[1]
    copies = []
    for k in range(count_k):
        for j in range(count_j):
            for t in range(2):
                row = pl.multiple_of((e ^ (2 * j + t)) * half, 16)
                weight[k, pl.ds(row, half), :] = pieces[j * count_k + k][t * half : (t + 1) * half, :]
        result[k] = jnp.dot(sel_ref[...], weight[k], preferred_element_type=f32).astype(bf16)
        at = pl.multiple_of((d ^ k) * columns, 128)
        copy = pltpu.make_async_copy(result.at[k], out_ref.at[:, pl.ds(at, columns)], sems.at[k])
        copy.start()
        copies.append(copy)
    for copy in copies:
        copy.wait()


def multiply(place, selected, pieces):
    count_j, count_k = len(pieces), len(pieces[0])
    rows, hidden = selected.shape
    columns = pieces[0][0].shape[1]
    flat = [v for group in pieces for v in group]
    vmem = pl.BlockSpec(memory_space=pltpu.VMEM)
    return pl.pallas_call(
        functools.partial(product_kernel, count_j, count_k),
        out_shape=jax.ShapeDtypeStruct((rows, columns * count_k), bf16),
        in_specs=[pl.BlockSpec(memory_space=pltpu.SMEM), vmem] + [vmem] * len(flat),
        out_specs=pl.BlockSpec(memory_space=pl.ANY),
        scratch_shapes=[
            pltpu.VMEM((count_k, hidden, columns), bf16),
            pltpu.VMEM((count_k, rows, columns), bf16),
            pltpu.SemaphoreType.DMA((count_k,)),
        ],
        compiler_params=pltpu.CompilerParams(vmem_limit_bytes=24 * 1024 * 1024),
    )(place, selected, *flat)


def step_kernel(place_ref, current_ref, next_ref, momentum_ref, master_ref, theirs_ref, *refs):
    count = theirs_ref.shape[0]
    kept, (new_ref, mine_ref, other_ref, totals, restored) = refs[:count], refs[count:]
    e = place_ref[0]
    rows = theirs_ref.shape[1]
    experts, _, columns = totals.shape
    totals[...] = jnp.zeros_like(totals)
    for q in range(2 * count):
        j, t = q // 2, q % 2
        piece = theirs_ref[j] if t else kept[j][:rows, :]
        x = current_ref[e ^ q, 0]
        totals[x] += piece.astype(f32)
    for x in range(experts):
        new = momentum_decay * momentum_ref[x] + totals[x]
        new_ref[x] = new
        master = master_ref[x]
        weights = master - step_rate * new
        for b in range(columns // QBLOCK):
            part = slice(b * QBLOCK, (b + 1) * QBLOCK)
            top = jnp.max(jnp.abs(master[:, part]), axis=1, keepdims=True)
            scale = (top / range_limit + epsilon).astype(bf16).astype(f32)
            quant = jnp.clip(weights[:, part] / scale, -range_limit, range_limit).astype(bf16)
            restored[x, :, part] = (quant.astype(f32) * scale).astype(bf16)
    for q in range(2 * count):
        j, t = q // 2, q % 2
        out = other_ref if t else mine_ref
        out[j] = restored[next_ref[e ^ q, 0]]


def step(place, current_slots, next_slots, momentum, master, theirs, kept):
    smem = pl.BlockSpec(memory_space=pltpu.SMEM)
    vmem = pl.BlockSpec(memory_space=pltpu.VMEM)
    sent = jax.ShapeDtypeStruct(theirs.shape, bf16)
    return pl.pallas_call(
        step_kernel,
        out_shape=(jax.ShapeDtypeStruct(momentum.shape, f32), sent, sent),
        in_specs=[smem] * 3 + [vmem] * (3 + len(kept)),
        out_specs=(vmem,) * 3,
        scratch_shapes=[pltpu.VMEM(momentum.shape, f32), pltpu.VMEM(momentum.shape, bf16)],
        compiler_params=pltpu.CompilerParams(vmem_limit_bytes=16 * 1024 * 1024),
    )(place, current_slots, next_slots, momentum, master, theirs, *kept)


def plain_plan(slot_grads, momentum, master_weights, current_slots, next_slots):
    expert_count = lax.axis_size("expert")
    gradient = slot_grads[0, 0]
    hidden_rows = gradient.shape[0]
    slice_rows = hidden_rows // expert_count
    experts, columns = momentum.shape[1:]
    labels = jnp.arange(experts, dtype=jnp.int32)
    owner_table = current_slots[:, 0][None, :] == labels[:, None]
    summed = lax.psum_scatter(gradient, "dp", scatter_dimension=1, tiled=True)
    pieces = summed.reshape(expert_count, slice_rows, columns)
    received = lax.all_to_all(pieces, "expert", split_axis=0, concat_axis=0, tiled=True).astype(f32)
    totals = jnp.einsum("xs,spk->pxk", owner_table.astype(f32), received, precision=lax.Precision.HIGHEST)
    new_momentum = momentum_decay * momentum + totals
    weights = master_weights - step_rate * new_momentum
    blocks = weights.reshape(slice_rows, experts, columns // QBLOCK, QBLOCK)
    previous = master_weights.reshape(slice_rows, experts, columns // QBLOCK, QBLOCK)
    scales = (jnp.max(jnp.abs(previous), axis=3) / range_limit + epsilon).astype(bf16)
    scales = scales.astype(f32)[:, :, :, None]
    quantized = jnp.clip(blocks / scales, -range_limit, range_limit).astype(bf16)
    restored = (quantized.astype(f32) * scales).astype(bf16).reshape(slice_rows, experts, columns)
    chooser = (next_slots[:, 0][:, None] == labels[None, :]).astype(bf16)
    sent = jnp.einsum("sx,pxk->spk", chooser, restored, preferred_element_type=f32).astype(bf16)
    got = lax.all_to_all(sent, "expert", split_axis=0, concat_axis=0, tiled=True)
    weight = lax.all_gather(got.reshape(hidden_rows, columns), "dp", axis=1, tiled=True)
    return new_momentum, weight


def staged_shards(slot_grads, momentum, master_weights, current_slots, next_slots, live_counts, route_index, activations):
    ne = lax.axis_size("expert")
    nd = lax.axis_size("dp")
    e = lax.axis_index("expert")
    d = lax.axis_index("dp")
    grad = slot_grads[0, 0]
    hid = grad.shape[0]
    sr = hid // ne
    nx = momentum.shape[1]
    cols = momentum.shape[2]
    nj = ne // 2
    ob = lax.optimization_barrier
    place = jnp.stack([e, d])

    def after(value, *deps):
        return ob((value, *deps))[0]

    def dperm(v, k):
        return lax.ppermute(v, "dp", [(i, i ^ k) for i in range(nd)])

    def eperm(v, q):
        return lax.ppermute(v, "expert", [(i, i ^ q) for i in range(ne)])

    def blk(js, ks, g):
        return jnp.concatenate(
            [lax.dynamic_slice(g, ((e ^ (2 * j + t)) * sr, (d ^ k) * cols), (sr, cols)) for k in ks for j in js for t in (0, 1)], 0
        )

    def add(*vs):
        out = vs[0].astype(f32)
        for v in vs[1:]:
            out = out + v.astype(f32)
        return out.astype(bf16)

    recv = {}
    n2 = 2 * sr
    far = (3, 2)
    fx, fy, fd = (blk(far, (k,), grad) for k in (1, 2, 3))
    grad = after(grad, fx, fy, fd)
    own_far = blk(far, (0,), grad)
    s1 = blk((1,), (1, 3), grad)
    s0 = blk((0,), (2, 3), grad)
    o1x, o1 = blk((1,), (2,), grad), blk((1,), (0,), grad)
    o0x, o0 = blk((0,), (1,), grad), blk((0,), (0,), grad)
    rfx = dperm(fx, 1)
    rfy = dperm(fy, 2)
    rfd = dperm(fd, 3)
    r1 = dperm(after(s1, rfx), 1)
    r0 = dperm(after(s0, rfy), 2)
    tfar = add(own_far, rfx, rfy, rfd)
    z3 = eperm(tfar[:n2], 6)
    z2 = eperm(tfar[n2:], 4)
    q1 = dperm(after(add(o1x, r1[n2:]), tfar), 2)
    q0 = dperm(after(add(o0x, r0[n2:]), tfar), 1)
    t1 = add(o1, r1[:n2], q1)
    z1 = eperm(after(t1, z3), 2)
    t0 = add(o0, r0[:n2], q0)
    recv = {0: t0, 1: z1, 2: z2, 3: z3}
    mom_t, mas_t = momentum.transpose(1, 0, 2), master_weights.transpose(1, 0, 2)
    theirs = eperm(jnp.stack([recv[j][sr:] for j in range(nj)]), 1)
    new_mom, mine, other = step(place, current_slots, next_slots, mom_t, mas_t, theirs, [recv[j] for j in range(nj)])
    got = eperm(other, 1)
    w = [jnp.concatenate([mine[j], got[j]], 0) for j in range(nj)]
    v = [w[0]] + [eperm(w[j], 2 * j) for j in (1, 2, 3)]
    ox = dperm(v[0], 1)
    y1 = dperm(v[1], 2)
    oy = dperm(jnp.concatenate([after(v[0], ox), ox], 0), 2)
    x1 = dperm(jnp.concatenate([after(v[1], y1), y1], 0), 1)
    vf = jnp.concatenate([v[2], v[3]], 0)
    gx = dperm(after(vf, x1), 1)
    gy = dperm(after(vf, oy), 2)
    gd = dperm(after(vf, oy, x1), 3)
    full = [
        [v[0], ox, oy[:n2], oy[n2:]],
        [v[1], x1[:n2], y1, x1[n2:]],
        [v[2], gx[:n2], gy[:n2], gd[:n2]],
        [v[3], gx[n2:], gy[n2:], gd[n2:]],
    ]
    new_mom = after(new_mom, ox)
    sel = select_rows(activations[0, 0], route_index[0, 0], live_counts)
    out = multiply(place, sel, full)
    return new_mom.transpose(1, 0, 2), out[None, None]


def plain_shards(slot_grads, momentum, master_weights, current_slots, next_slots, live_counts, route_index, activations):
    new_momentum, weight = plain_plan(slot_grads, momentum, master_weights, current_slots, next_slots)
    selected = select_rows(activations[0, 0], route_index[0, 0], live_counts)
    product = jnp.dot(selected, weight, preferred_element_type=f32)
    return new_momentum, product.astype(bf16)[None, None]


def solution(mesh):
    in_specs = (
        P("dp", "expert", None, None), P("expert", None, "dp"), P("expert", None, "dp"), P(), P(), P("dp", "expert"),
        P("dp", "expert", None, None), P("dp", "expert", None, None),
    )
    out_specs = (P("expert", None, "dp"), P("dp", "expert", None, None))
    staged = mesh.shape["dp"] == 4 and mesh.shape["expert"] == 8
    shards = staged_shards if staged else plain_shards
    return jax.shard_map(shards, mesh=mesh, in_specs=in_specs, out_specs=out_specs, check_vma=False)
```

```python
import functools

import jax
import jax.numpy as jnp
from jax import lax
from jax.experimental import pallas as pl
from jax.experimental.pallas import tpu as pltpu
from jax.sharding import PartitionSpec as P

QBLOCK = 128
momentum_decay = 0.9
step_rate = 0.5
epsilon = 1e-06
range_limit = 448.0
f32, bf16 = jnp.float32, jnp.bfloat16


def select_kernel(live_ref, index_ref, act_ref, out_ref):
    blocks, size = index_ref.shape
    for q in range(blocks):
        rows = lax.broadcasted_iota(jnp.int32, (size, size), 0)
        hot = (rows == index_ref[q : q + 1, :]).astype(f32).astype(bf16)
        picked = lax.dot_general(
            hot, act_ref[q * size : (q + 1) * size, :], (((0,), (0,)), ((), ())), preferred_element_type=f32
        )
        at = lax.broadcasted_iota(jnp.int32, picked.shape, 0) + q * size
        out_ref[q * size : (q + 1) * size, :] = jnp.where(at < live_ref[0, 0], picked, 0.0).astype(bf16)


def select_rows(activations, route_index, live_counts):
    rows, hidden = activations.shape
    return pl.pallas_call(
        select_kernel,
        out_shape=jax.ShapeDtypeStruct((rows, hidden), bf16),
        in_specs=[
            pl.BlockSpec(memory_space=pltpu.SMEM),
            pl.BlockSpec(memory_space=pltpu.VMEM),
            pl.BlockSpec(memory_space=pltpu.VMEM),
        ],
        out_specs=pl.BlockSpec(memory_space=pltpu.VMEM),
    )(live_counts, route_index, activations)


def product_kernel(count_j, count_k, place_ref, sel_ref, *refs):
    pieces = refs[: count_j * count_k]
    out_ref, weight, result, sems = refs[count_j * count_k :]
    e, d = place_ref[0], place_ref[1]
    half = pieces[0].shape[0] // 2
    columns = pieces[0].shape[1]
    copies = []
    for k in range(count_k):
        for j in range(count_j):
            for t in range(2):
                row = pl.multiple_of((e ^ (2 * j + t)) * half, 16)
                weight[k, pl.ds(row, half), :] = pieces[j * count_k + k][t * half : (t + 1) * half, :]
        result[k] = jnp.dot(sel_ref[...], weight[k], preferred_element_type=f32).astype(bf16)
        at = pl.multiple_of((d ^ k) * columns, 128)
        copy = pltpu.make_async_copy(result.at[k], out_ref.at[:, pl.ds(at, columns)], sems.at[k])
        copy.start()
        copies.append(copy)
    for copy in copies:
        copy.wait()


def multiply(place, selected, pieces):
    count_j, count_k = len(pieces), len(pieces[0])
    rows, hidden = selected.shape
    columns = pieces[0][0].shape[1]
    flat = [v for group in pieces for v in group]
    vmem = pl.BlockSpec(memory_space=pltpu.VMEM)
    return pl.pallas_call(
        functools.partial(product_kernel, count_j, count_k),
        out_shape=jax.ShapeDtypeStruct((rows, columns * count_k), bf16),
        in_specs=[pl.BlockSpec(memory_space=pltpu.SMEM), vmem] + [vmem] * len(flat),
        out_specs=pl.BlockSpec(memory_space=pl.ANY),
        scratch_shapes=[
            pltpu.VMEM((count_k, hidden, columns), bf16),
            pltpu.VMEM((count_k, rows, columns), bf16),
            pltpu.SemaphoreType.DMA((count_k,)),
        ],
        compiler_params=pltpu.CompilerParams(vmem_limit_bytes=24 * 1024 * 1024),
    )(place, selected, *flat)


def step_kernel(place_ref, current_ref, next_ref, momentum_ref, master_ref, theirs_ref, *refs):
    count = theirs_ref.shape[0]
    kept, (new_ref, mine_ref, other_ref, totals, restored) = refs[:count], refs[count:]
    e = place_ref[0]
    rows = theirs_ref.shape[1]
    experts, _, columns = totals.shape
    totals[...] = jnp.zeros_like(totals)
    for q in range(2 * count):
        j, t = q // 2, q % 2
        piece = theirs_ref[j] if t else kept[j][:rows, :]
        x = current_ref[e ^ q, 0]
        totals[x] += piece.astype(f32)
    for x in range(experts):
        new = momentum_decay * momentum_ref[x] + totals[x]
        new_ref[x] = new
        master = master_ref[x]
        weights = master - step_rate * new
        for b in range(columns // QBLOCK):
            part = slice(b * QBLOCK, (b + 1) * QBLOCK)
            top = jnp.max(jnp.abs(master[:, part]), axis=1, keepdims=True)
            scale = (top / range_limit + epsilon).astype(bf16).astype(f32)
            quant = jnp.clip(weights[:, part] / scale, -range_limit, range_limit).astype(bf16)
            restored[x, :, part] = (quant.astype(f32) * scale).astype(bf16)
    for q in range(2 * count):
        j, t = q // 2, q % 2
        out = other_ref if t else mine_ref
        out[j] = restored[next_ref[e ^ q, 0]]


def step(place, current_slots, next_slots, momentum, master, theirs, kept):
    smem = pl.BlockSpec(memory_space=pltpu.SMEM)
    vmem = pl.BlockSpec(memory_space=pltpu.VMEM)
    sent = jax.ShapeDtypeStruct(theirs.shape, bf16)
    return pl.pallas_call(
        step_kernel,
        out_shape=(jax.ShapeDtypeStruct(momentum.shape, f32), sent, sent),
        in_specs=[smem] * 3 + [vmem] * (3 + len(kept)),
        out_specs=(vmem,) * 3,
        scratch_shapes=[pltpu.VMEM(momentum.shape, f32), pltpu.VMEM(momentum.shape, bf16)],
        compiler_params=pltpu.CompilerParams(vmem_limit_bytes=16 * 1024 * 1024),
    )(place, current_slots, next_slots, momentum, master, theirs, *kept)


def plain_plan(slot_grads, momentum, master_weights, current_slots, next_slots):
    expert_count = lax.axis_size("expert")
    gradient = slot_grads[0, 0]
    hidden_rows = gradient.shape[0]
    slice_rows = hidden_rows // expert_count
    experts, columns = momentum.shape[1:]
    labels = jnp.arange(experts, dtype=jnp.int32)
    owner_table = current_slots[:, 0][None, :] == labels[:, None]
    summed = lax.psum_scatter(gradient, "dp", scatter_dimension=1, tiled=True)
    pieces = summed.reshape(expert_count, slice_rows, columns)
    received = lax.all_to_all(pieces, "expert", split_axis=0, concat_axis=0, tiled=True).astype(f32)
    totals = jnp.einsum("xs,spk->pxk", owner_table.astype(f32), received, precision=lax.Precision.HIGHEST)
    new_momentum = momentum_decay * momentum + totals
    weights = master_weights - step_rate * new_momentum
    blocks = weights.reshape(slice_rows, experts, columns // QBLOCK, QBLOCK)
    previous = master_weights.reshape(slice_rows, experts, columns // QBLOCK, QBLOCK)
    scales = (jnp.max(jnp.abs(previous), axis=3) / range_limit + epsilon).astype(bf16)
    scales = scales.astype(f32)[:, :, :, None]
    quantized = jnp.clip(blocks / scales, -range_limit, range_limit).astype(bf16)
    restored = (quantized.astype(f32) * scales).astype(bf16).reshape(slice_rows, experts, columns)
    chooser = (next_slots[:, 0][:, None] == labels[None, :]).astype(bf16)
    sent = jnp.einsum("sx,pxk->spk", chooser, restored, preferred_element_type=f32).astype(bf16)
    got = lax.all_to_all(sent, "expert", split_axis=0, concat_axis=0, tiled=True)
    weight = lax.all_gather(got.reshape(hidden_rows, columns), "dp", axis=1, tiled=True)
    return new_momentum, weight


def staged_shards(slot_grads, momentum, master_weights, current_slots, next_slots, live_counts, route_index, activations):
    ne = lax.axis_size("expert")
    nd = lax.axis_size("dp")
    e = lax.axis_index("expert")
    d = lax.axis_index("dp")
    grad = slot_grads[0, 0]
    hid = grad.shape[0]
    sr = hid // ne
    nx = momentum.shape[1]
    cols = momentum.shape[2]
    nj = ne // 2
    n2 = 2 * sr
    ob = lax.optimization_barrier
    place = jnp.stack([e, d])

    def after(value, *deps):
        return ob((value, *deps))[0]

    def dperm(v, k):
        return lax.ppermute(v, "dp", [(i, i ^ k) for i in range(nd)])

    def eperm(v, q):
        return lax.ppermute(v, "expert", [(i, i ^ q) for i in range(ne)])

    def blk(js, ks, g):
        return jnp.concatenate(
            [lax.dynamic_slice(g, ((e ^ (2 * j + t)) * sr, (d ^ k) * cols), (sr, cols)) for k in ks for j in js for t in (0, 1)], 0
        )

    def add(*vs):
        out = vs[0].astype(f32)
        for v in vs[1:]:
            out = out + v.astype(f32)
        return out.astype(bf16)

    sx3 = blk((3,), (1, 3), grad)
    sy2 = blk((2,), (2, 3), grad)
    grad = after(grad, sx3, sy2)
    ox3, o3 = blk((3,), (2,), grad), blk((3,), (0,), grad)
    oy2, o2 = blk((2,), (1,), grad), blk((2,), (0,), grad)
    sx1 = blk((1,), (1, 3), grad)
    sy0 = blk((0,), (2, 3), grad)
    ox1, o1 = blk((1,), (2,), grad), blk((1,), (0,), grad)
    oy0, o0 = blk((0,), (1,), grad), blk((0,), (0,), grad)
    x3 = dperm(sx3, 1)
    y2 = dperm(sy2, 2)
    x1 = dperm(sx1, 1)
    y0 = dperm(sy0, 2)
    y3 = dperm(add(ox3, x3[n2:]), 2)
    x2 = dperm(add(oy2, y2[n2:]), 1)
    t3 = add(o3, x3[:n2], y3)
    t2 = add(o2, y2[:n2], x2)
    z3 = eperm(t3, 6)
    z2 = eperm(t2, 4)
    y1 = dperm(add(ox1, x1[n2:]), 2)
    x0 = dperm(add(oy0, y0[n2:]), 1)
    t1 = add(o1, x1[:n2], y1)
    z1 = eperm(t1, 2)
    t0 = add(after(o0, z3, z2), y0[:n2], x0)
    recv = {0: t0, 1: z1, 2: z2, 3: z3}
    mom_t, mas_t = momentum.transpose(1, 0, 2), master_weights.transpose(1, 0, 2)
    theirs = eperm(jnp.stack([recv[j][sr:] for j in range(nj)]), 1)
    new_mom, mine, other = step(place, current_slots, next_slots, mom_t, mas_t, theirs, [recv[j] for j in range(nj)])
    got = eperm(other, 1)
    w = [jnp.concatenate([mine[j], got[j]], 0) for j in range(nj)]
    v = [w[0], None, None, None]
    v[1] = eperm(w[1], 2)
    v[2] = eperm(w[2], 4)
    v[3] = eperm(w[3], 6)
    full = [None] * 4
    ax0 = dperm(v[0], 1)
    by0 = dperm(v[1], 2)
    ay0 = dperm(jnp.concatenate([v[0], ax0], 0), 2)
    bx0 = dperm(jnp.concatenate([v[1], by0], 0), 1)
    full[0] = [v[0], ax0, ay0[:n2], ay0[n2:]]
    full[1] = [v[1], bx0[:n2], by0, bx0[n2:]]
    ax1 = dperm(v[2], 1)
    by1 = dperm(v[3], 2)
    ay1 = dperm(jnp.concatenate([v[2], ax1], 0), 2)
    bx1 = dperm(jnp.concatenate([v[3], by1], 0), 1)
    full[2] = [v[2], ax1, ay1[:n2], ay1[n2:]]
    full[3] = [v[3], bx1[:n2], by1, bx1[n2:]]
    late = ay0
    new_mom = after(new_mom, late)
    sel = select_rows(activations[0, 0], route_index[0, 0], live_counts)
    out = multiply(place, sel, full)
    return new_mom.transpose(1, 0, 2), out[None, None]


def plain_shards(slot_grads, momentum, master_weights, current_slots, next_slots, live_counts, route_index, activations):
    new_momentum, weight = plain_plan(slot_grads, momentum, master_weights, current_slots, next_slots)
    selected = select_rows(activations[0, 0], route_index[0, 0], live_counts)
    product = jnp.dot(selected, weight, preferred_element_type=f32)
    return new_momentum, product.astype(bf16)[None, None]


def solution(mesh):
    in_specs = (
        P("dp", "expert", None, None), P("expert", None, "dp"), P("expert", None, "dp"), P(), P(), P("dp", "expert"),
        P("dp", "expert", None, None), P("dp", "expert", None, None),
    )
    out_specs = (P("expert", None, "dp"), P("dp", "expert", None, None))
    staged = mesh.shape["dp"] == 4 and mesh.shape["expert"] == 8
    shards = staged_shards if staged else plain_shards
    return jax.shard_map(shards, mesh=mesh, in_specs=in_specs, out_specs=out_specs, check_vma=False)
```

```python
import functools

import jax
import jax.numpy as jnp
from jax import lax
from jax.experimental import pallas as pl
from jax.experimental.pallas import tpu as pltpu
from jax.sharding import PartitionSpec as P

QBLOCK = 128
momentum_decay = 0.9
step_rate = 0.5
epsilon = 1e-06
range_limit = 448.0
f32, bf16 = jnp.float32, jnp.bfloat16


def select_kernel(live_ref, index_ref, act_ref, out_ref):
    blocks, size = index_ref.shape
    for q in range(blocks):
        rows = lax.broadcasted_iota(jnp.int32, (size, size), 0)
        hot = (rows == index_ref[q : q + 1, :]).astype(f32).astype(bf16)
        picked = lax.dot_general(
            hot, act_ref[q * size : (q + 1) * size, :], (((0,), (0,)), ((), ())), preferred_element_type=f32
        )
        at = lax.broadcasted_iota(jnp.int32, picked.shape, 0) + q * size
        out_ref[q * size : (q + 1) * size, :] = jnp.where(at < live_ref[0, 0], picked, 0.0).astype(bf16)


def select_rows(activations, route_index, live_counts):
    rows, hidden = activations.shape
    return pl.pallas_call(
        select_kernel,
        out_shape=jax.ShapeDtypeStruct((rows, hidden), bf16),
        in_specs=[
            pl.BlockSpec(memory_space=pltpu.SMEM),
            pl.BlockSpec(memory_space=pltpu.VMEM),
            pl.BlockSpec(memory_space=pltpu.VMEM),
        ],
        out_specs=pl.BlockSpec(memory_space=pltpu.VMEM),
    )(live_counts, route_index, activations)


def product_kernel(where, steps, started, place_ref, sel_ref, *refs):
    refs = refs[1:] if started else refs
    refs, (out_ref, weight, result, sems) = refs[:-4], refs[-4:]
    e, d = place_ref[0], place_ref[1]
    _, hidden, columns = weight.shape
    half = hidden // len(where) // 2
    tall = result.shape[1] // 2
    copies = []
    for n, k in enumerate(steps):
        for j, places in enumerate(where):
            ref, offset = refs[places[n][0]], places[n][1]
            for t in range(2):
                at = pl.multiple_of((e ^ (2 * j + t)) * half, 16)
                weight[n, pl.ds(at, half), :] = ref[offset + t * half : offset + (t + 1) * half, :]
        at = pl.multiple_of((d ^ k) * columns, 128)
        for m in range(2):
            part = slice(m * tall, (m + 1) * tall)
            result[n, part] = jnp.dot(sel_ref[part, :], weight[n], preferred_element_type=f32).astype(bf16)
            copy = pltpu.make_async_copy(
                result.at[n, pl.ds(m * tall, tall), :],
                out_ref.at[pl.ds(m * tall, tall), pl.ds(at, columns)],
                sems.at[2 * n + m],
            )
            copy.start()
            copies.append(copy)
    for copy in copies:
        copy.wait()


def multiply(place, selected, pieces, steps, total, begun=None):
    arrays, where = [], []
    for group in pieces:
        where.append([])
        for array, offset in group:
            found = [n for n, other in enumerate(arrays) if other is array]
            if not found:
                arrays.append(array)
            where[-1].append((found[0] if found else len(arrays) - 1, offset))
    rows, hidden = selected.shape
    columns = arrays[0].shape[1]
    vmem, anywhere = pl.BlockSpec(memory_space=pltpu.VMEM), pl.BlockSpec(memory_space=pl.ANY)
    first = () if begun is None else (begun,)
    return pl.pallas_call(
        functools.partial(product_kernel, where, steps, bool(first)),
        out_shape=jax.ShapeDtypeStruct((rows, columns * total), bf16),
        in_specs=[pl.BlockSpec(memory_space=pltpu.SMEM), vmem] + [anywhere] * len(first) + [vmem] * len(arrays),
        out_specs=anywhere,
        scratch_shapes=[
            pltpu.VMEM((len(steps), hidden, columns), bf16),
            pltpu.VMEM((len(steps), rows, columns), bf16),
            pltpu.SemaphoreType.DMA((2 * len(steps),)),
        ],
        input_output_aliases={2: 0} if first else {},
        compiler_params=pltpu.CompilerParams(vmem_limit_bytes=24 * 1024 * 1024),
    )(place, selected, *first, *arrays)


def step_kernel(place_ref, current_ref, next_ref, momentum_ref, master_ref, theirs_ref, *refs):
    count = theirs_ref.shape[0]
    kept, (new_ref, mine_ref, other_ref, totals, restored) = refs[:count], refs[count:]
    e = place_ref[0]
    rows = theirs_ref.shape[1]
    experts, _, columns = totals.shape
    totals[...] = jnp.zeros_like(totals)
    for q in range(2 * count):
        j, t = q // 2, q % 2
        piece = theirs_ref[j] if t else kept[j][:rows, :]
        x = current_ref[e ^ q, 0]
        totals[x] += piece.astype(f32)
    for x in range(experts):
        new = momentum_decay * momentum_ref[x] + totals[x]
        new_ref[x] = new
        master = master_ref[x]
        weights = master - step_rate * new
        for b in range(columns // QBLOCK):
            part = slice(b * QBLOCK, (b + 1) * QBLOCK)
            top = jnp.max(jnp.abs(master[:, part]), axis=1, keepdims=True)
            scale = (top / range_limit + epsilon).astype(bf16).astype(f32)
            quant = jnp.clip(weights[:, part] / scale, -range_limit, range_limit).astype(bf16)
            restored[x, :, part] = (quant.astype(f32) * scale).astype(bf16)
    for q in range(2 * count):
        j, t = q // 2, q % 2
        out = other_ref if t else mine_ref
        out[j] = restored[next_ref[e ^ q, 0]]


def step(place, current_slots, next_slots, momentum, master, theirs, kept):
    smem = pl.BlockSpec(memory_space=pltpu.SMEM)
    vmem = pl.BlockSpec(memory_space=pltpu.VMEM)
    sent = jax.ShapeDtypeStruct(theirs.shape, bf16)
    return pl.pallas_call(
        step_kernel,
        out_shape=(jax.ShapeDtypeStruct(momentum.shape, f32), sent, sent),
        in_specs=[smem] * 3 + [vmem] * (3 + len(kept)),
        out_specs=(vmem,) * 3,
        scratch_shapes=[pltpu.VMEM(momentum.shape, f32), pltpu.VMEM(momentum.shape, bf16)],
        compiler_params=pltpu.CompilerParams(vmem_limit_bytes=16 * 1024 * 1024),
    )(place, current_slots, next_slots, momentum, master, theirs, *kept)


def plain_plan(slot_grads, momentum, master_weights, current_slots, next_slots):
    expert_count = lax.axis_size("expert")
    gradient = slot_grads[0, 0]
    hidden_rows = gradient.shape[0]
    slice_rows = hidden_rows // expert_count
    experts, columns = momentum.shape[1:]
    labels = jnp.arange(experts, dtype=jnp.int32)
    owner_table = current_slots[:, 0][None, :] == labels[:, None]
    summed = lax.psum_scatter(gradient, "dp", scatter_dimension=1, tiled=True)
    pieces = summed.reshape(expert_count, slice_rows, columns)
    received = lax.all_to_all(pieces, "expert", split_axis=0, concat_axis=0, tiled=True).astype(f32)
    totals = jnp.einsum("xs,spk->pxk", owner_table.astype(f32), received, precision=lax.Precision.HIGHEST)
    new_momentum = momentum_decay * momentum + totals
    weights = master_weights - step_rate * new_momentum
    blocks = weights.reshape(slice_rows, experts, columns // QBLOCK, QBLOCK)
    previous = master_weights.reshape(slice_rows, experts, columns // QBLOCK, QBLOCK)
    scales = (jnp.max(jnp.abs(previous), axis=3) / range_limit + epsilon).astype(bf16)
    scales = scales.astype(f32)[:, :, :, None]
    quantized = jnp.clip(blocks / scales, -range_limit, range_limit).astype(bf16)
    restored = (quantized.astype(f32) * scales).astype(bf16).reshape(slice_rows, experts, columns)
    chooser = (next_slots[:, 0][:, None] == labels[None, :]).astype(bf16)
    sent = jnp.einsum("sx,pxk->spk", chooser, restored, preferred_element_type=f32).astype(bf16)
    got = lax.all_to_all(sent, "expert", split_axis=0, concat_axis=0, tiled=True)
    weight = lax.all_gather(got.reshape(hidden_rows, columns), "dp", axis=1, tiled=True)
    return new_momentum, weight


def staged_shards(slot_grads, momentum, master_weights, current_slots, next_slots, live_counts, route_index, activations):
    ne = lax.axis_size("expert")
    nd = lax.axis_size("dp")
    e = lax.axis_index("expert")
    d = lax.axis_index("dp")
    grad = slot_grads[0, 0]
    hid = grad.shape[0]
    sr = hid // ne
    nx = momentum.shape[1]
    cols = momentum.shape[2]
    nj = ne // 2
    n2 = 2 * sr
    ob = lax.optimization_barrier
    place = jnp.stack([e, d])

    def after(value, *deps):
        return ob((value, *deps))[0]

    def dperm(v, k):
        return lax.ppermute(v, "dp", [(i, i ^ k) for i in range(nd)])

    def eperm(v, q):
        return lax.ppermute(v, "expert", [(i, i ^ q) for i in range(ne)])

    def blk(js, ks, g):
        return jnp.concatenate(
            [lax.dynamic_slice(g, ((e ^ (2 * j + t)) * sr, (d ^ k) * cols), (sr, cols)) for k in ks for j in js for t in (0, 1)], 0
        )

    def add(*vs):
        out = vs[0].astype(f32)
        for v in vs[1:]:
            out = out + v.astype(f32)
        return out.astype(bf16)

    sel = select_rows(activations[0, 0], route_index[0, 0], live_counts)
    sx3 = blk((3,), (1, 3), grad)
    sy2 = blk((2,), (2, 3), grad)
    grad = after(grad, sx3, sy2)
    ox3, o3 = blk((3,), (2,), grad), blk((3,), (0,), grad)
    oy2, o2 = blk((2,), (1,), grad), blk((2,), (0,), grad)
    sx1 = blk((1,), (1, 3), grad)
    sy0 = blk((0,), (2, 3), grad)
    ox1, o1 = blk((1,), (2,), grad), blk((1,), (0,), grad)
    oy0, o0 = blk((0,), (1,), grad), blk((0,), (0,), grad)
    x3 = dperm(sx3, 1)
    y2 = dperm(sy2, 2)
    y3 = dperm(after(add(ox3, x3[n2:]), sel), 2)
    x2 = dperm(add(oy2, y2[n2:]), 1)
    x1 = dperm(sx1, 1)
    y0 = dperm(after(sy0, y2), 2)
    y1 = dperm(add(ox1, x1[n2:]), 2)
    t3 = add(o3, x3[:n2], y3)
    t2 = add(o2, y2[:n2], x2)
    z2 = eperm(t2, 4)
    z3 = eperm(t3, 6)
    t1 = add(o1, x1[:n2], y1)
    z1 = eperm(t1, 2)
    x0 = dperm(add(oy0, y0[n2:]), 1)
    t0 = add(after(o0, z3, z2), y0[:n2], x0)
    recv = {0: t0, 1: z1, 2: z2, 3: z3}
    mom_t, mas_t = momentum.transpose(1, 0, 2), master_weights.transpose(1, 0, 2)
    theirs = eperm(jnp.stack([recv[j][sr:] for j in range(nj)]), 1)
    new_mom, mine, other = step(place, current_slots, next_slots, mom_t, mas_t, theirs, [recv[j] for j in range(nj)])
    got = eperm(other, 1)
    w = [jnp.concatenate([mine[j], got[j]], 0) for j in range(nj)]
    v = [w[0], None, None, None]
    v[2] = eperm(w[2], 4)
    v[3] = eperm(w[3], 6)
    v[1] = eperm(w[1], 2)
    ax = dperm(v[0], 1)
    by = dperm(v[1], 2)
    ay = dperm(jnp.concatenate([v[0], ax], 0), 2)
    bx = dperm(jnp.concatenate([v[1], by], 0), 1)
    cx = dperm(v[2], 1)
    ey = dperm(v[3], 2)
    cy = dperm(jnp.concatenate([v[2], cx], 0), 2)
    ex = dperm(jnp.concatenate([v[3], ey], 0), 1)
    pieces = [
        [(v[0], 0), (ax, 0), (ay, 0), (ay, n2)],
        [(v[1], 0), (bx, 0), (by, 0), (bx, n2)],
        [(v[2], 0), (cx, 0), (cy, 0), (cy, n2)],
        [(v[3], 0), (ex, 0), (ey, 0), (ex, n2)],
    ]
    late = ay
    new_mom = after(new_mom, late)
    begun = multiply(place, sel, [group[:1] for group in pieces], (0,), nd)
    out = multiply(place, sel, [group[1:] for group in pieces], (1, 2, 3), nd, begun)
    return new_mom.transpose(1, 0, 2), out[None, None]


def plain_shards(slot_grads, momentum, master_weights, current_slots, next_slots, live_counts, route_index, activations):
    new_momentum, weight = plain_plan(slot_grads, momentum, master_weights, current_slots, next_slots)
    selected = select_rows(activations[0, 0], route_index[0, 0], live_counts)
    product = jnp.dot(selected, weight, preferred_element_type=f32)
    return new_momentum, product.astype(bf16)[None, None]


def solution(mesh):
    in_specs = (
        P("dp", "expert", None, None), P("expert", None, "dp"), P("expert", None, "dp"), P(), P(), P("dp", "expert"),
        P("dp", "expert", None, None), P("dp", "expert", None, None),
    )
    out_specs = (P("expert", None, "dp"), P("dp", "expert", None, None))
    staged = mesh.shape["dp"] == 4 and mesh.shape["expert"] == 8
    shards = staged_shards if staged else plain_shards
    return jax.shard_map(shards, mesh=mesh, in_specs=in_specs, out_specs=out_specs, check_vma=False)
```
